32 devices in a mesh: tile: 16 (over z, y, x), rhs: 2 (over core).
Axes of the slice: x: 2, y: 2, z: 4, core: 2. Of those that a mesh axis runs over, the one named last changes fastest.
Arguments:
- sensitivity: bfloat16 [16384, 5120], P('tile', 'rhs'), may hold values from -0.0625 to 0.0625
- precision: float32 [5120], P('rhs'), may hold values from 3 to 60
- reaction: float32 [128, 128], P('tile'), may hold values from 0.25 to 2
- load: float32 [64, 16384], P(None, 'tile'), may hold values from -24 to 24
Outputs:
- solution: float32 [64, 16384], P(None, 'tile')
- residual: float32 [64, 16384], P(None, 'tile')
The draws below stay inside these ranges and needn't reach their ends.
All inputs are finite; a program needn't handle non-finite values.
Results may differ from the reference program's by a relative error of at most 0.0042.
Values may be sent and summed in bfloat16 or wider, within the bound.
A program may use at most 64 MiB of HBM per device.

```python
import math
import jax
import jax.numpy as jnp
from jax import lax

GY = 128
RHS = 64
ITERS = 2
NX = 128
PARAMS = 16384
OBS = 5120


def with_spikes(entries, key, source, target, blocks, factor):
    def block_of(dim):
        return (jnp.arange(entries.shape[dim]) // (entries.shape[dim] // blocks)).reshape((-1,) + (1,) * (entries.ndim - 1 - dim))

    first = jax.random.permutation(key, blocks)[block_of(target)]
    other_side = (block_of(target) + blocks // 2) % blocks
    return jnp.where((block_of(source) == first) | (block_of(source) == other_side), factor * entries, entries)


def shard_levels(own_key, shape, split, smallest, top_value):
    factor_of, own = 1.0, jax.random.fold_in(own_key, 6)
    for dim, blocks in split:
        steps = jnp.exp(jax.random.uniform(jax.random.fold_in(own, dim), (blocks,), jnp.float32, smallest / len(split), top_value / len(split)))
        factor_of = factor_of * jnp.repeat(steps, shape[dim] // blocks).reshape([-1 if axis == dim else 1 for axis in range(len(shape))])
    return factor_of


def noise(stream_key, shape, deviation, most, split=(), kind=jnp.bfloat16):
    drawn = deviation * jax.random.normal(stream_key, shape, jnp.float32)
    if split:
        drawn = drawn * shard_levels(stream_key, shape, split, -0.22, 0.18)
    return jnp.clip(drawn, -most, most).astype(kind)


def noise_with(rng, shape, scale, bound, shards, heavy, held_as=jnp.bfloat16):
    values = scale * jax.random.normal(rng, shape, jnp.float32)
    if shards:
        values = values * shard_levels(rng, shape, shards, -0.22, 0.18)
    return jnp.clip(with_spikes(values, jax.random.fold_in(rng, 3), *heavy), -bound, bound).astype(held_as)


def setup_inputs(seed: int = 0) -> dict:
    arg_keys = jax.random.split(jax.random.key(seed), 5)
    sensitivity = noise_with(arg_keys[0], (PARAMS, OBS), PARAMS ** -0.5, 0.0625, ((0, 16), (1, 2)), (0, 1, 16, 2.0))
    precision = jnp.clip(jnp.exp(math.log(60.0) - 2.9957323 * jax.random.uniform(arg_keys[1], (OBS,), jnp.float32) ** shard_levels(arg_keys[1], (OBS,), ((0, 2),), -0.2, 0.2)), 3.0, 60.0)
    reaction = jnp.clip(jnp.exp(math.log(2.0) - 2.0794415 * jax.random.uniform(arg_keys[2], (NX, GY), jnp.float32) ** shard_levels(arg_keys[2], (NX, GY), ((0, 16),), -0.2, 0.2)), 0.25, 2.0)
    load = noise(arg_keys[3], (RHS, PARAMS), 4.0, 24.0, ((1, 16),), jnp.float32)
    return {"sensitivity": sensitivity, "precision": precision, "reaction": reaction, "load": load}


def apply_stencil(field, reaction):
    padded = jnp.pad(field, ((0, 0), (1, 1), (1, 1)))
    neighbours = padded[:, 2:, 1:-1] + padded[:, :-2, 1:-1] + padded[:, 1:-1, 2:] + padded[:, 1:-1, :-2]
    return (reaction + 4.0) * field - neighbours


def hessian(direction, sensitivity, precision, reaction):
    lowered = direction.astype(jnp.bfloat16)
    predicted = jnp.dot(lowered, sensitivity, preferred_element_type=jnp.float32)
    weighted = (precision[None, :] * predicted).astype(jnp.bfloat16)
    back = lax.dot_general(weighted, sensitivity, (((1,), (1,)), ((), ())), preferred_element_type=jnp.float32)
    grid = direction.reshape(direction.shape[0], reaction.shape[0], reaction.shape[1])
    twice = apply_stencil(apply_stencil(grid, reaction), reaction)
    return back + twice.reshape(direction.shape)


def reference(sensitivity, precision, reaction, load):
    solution = jnp.zeros_like(load)
    residual = load
    direction = load
    current = jnp.sum(residual * residual, axis=1)
    for iteration in range(ITERS):
        image = hessian(direction, sensitivity, precision, reaction)
        alpha = current / jnp.sum(direction * image, axis=1)
        solution = solution + alpha[:, None] * direction
        residual = residual - alpha[:, None] * image
        if iteration + 1 < ITERS:
            fresh = jnp.sum(residual * residual, axis=1)
            direction = residual + (fresh / current)[:, None] * direction
            current = fresh
    return solution, residual
```

```python
import functools

import jax
import jax.numpy as jnp
from jax import lax
from jax.experimental import pallas as pl
from jax.experimental.pallas import tpu as pltpu
from jax.sharding import PartitionSpec as P

ITERS = 2
LANES = 128
ROWS16 = 16
SPLIT = (3, 2)
F32, BF16 = jnp.float32, jnp.bfloat16


def lane_ids(rows):
    return lax.broadcasted_iota(jnp.int32, (rows, LANES), 1)


def encode(value):
    high = value.astype(BF16).astype(F32)
    lanes = lax.broadcasted_iota(jnp.int32, value.shape, value.ndim - 1)
    return jnp.where(lanes < LANES // 2, high, value - high).astype(BF16)


def decode(piece):
    wide = piece.astype(F32)
    return wide + pltpu.roll(wide, LANES // 2, wide.ndim - 1)


def spread(rows, columns):
    lanes = lane_ids(rows) % (LANES // 2)
    out = jnp.zeros((rows, LANES), F32)
    for lane, column in columns.items():
        out = jnp.where(lanes == lane, column, out)
    return out


def kernel(
    n, chunks, sens_hbm, prec_hbm, reaction_hbm, load_hbm, sol_out, res_out,
    sens, prec, reaction, load, react_in, halo, field1, efield, eetwice,
    pred32, send_a, recv_a, sum_z, send_z, recv_z, pred0, wb, core_send, core_recv, scal,
    esend_a, erecv_a, esend_z, erecv_z, efull,
    load_sem, sems_s, sems_r, halo_s, halo_r, react_s, react_r, core_s, core_r, e_s, e_r,
):
    t = lax.axis_index("tile")
    r = lax.axis_index("rhs")
    rz = n // 4
    x, y, z, g = t % 2, (t // 2) % 2, t // 4, t % 4
    steps_xy = (3 - 2 * x - 4 * y, 1 - 2 * x, 2 - 4 * y)
    count, strip = load.shape
    half = count // 2
    rows = reaction.shape[0]
    obs = sens.shape[1]
    total = sum(chunks) * rz * LANES
    last = len(chunks) - 1
    has_low, has_high = t > 0, t < n - 1

    def to(tile):
        return (tile, r)

    small = []
    for at, (src, dst) in enumerate(((load_hbm, load), (prec_hbm, prec), (reaction_hbm, reaction))):
        copy = pltpu.make_async_copy(src, dst, load_sem.at[len(chunks) + at])
        copy.start()
        small.append(copy)
    starts = [sum(chunks[:c]) for c in range(len(chunks))]
    spans = []
    loads = []
    for c, u in enumerate(chunks):
        lo = min(starts[c] * rz * LANES, obs)
        hi = min((starts[c] + u) * rz * LANES, obs)
        spans.append((lo, hi))
        copy = pltpu.make_async_copy(
            sens_hbm.at[:, lo:hi], sens.at[:, lo:hi], load_sem.at[c]
        )
        copy.start()
        loads.append(copy)

    barrier = pltpu.get_barrier_semaphore()

    def greet(device):
        pl.semaphore_signal(
            barrier, inc=1, device_id=device, device_id_type=pl.DeviceIdType.MESH
        )

    greet((t, 1 - r))
    xy_peers = [t + step for step in steps_xy]
    z_peers = [((z + k) % rz) * 4 + g for k in range(1, rz)]
    for peer in xy_peers + z_peers:
        greet(to(peer))

    @pl.when(has_low)
    def _():
        greet(to(t - 1))

    @pl.when(has_high)
    def _():
        greet(to(t + 1))

    @pl.when(jnp.logical_not(has_low))
    def _():
        for it in range(ITERS):
            halo[it, 0] = jnp.zeros(halo.shape[2:], F32)
        react_in[0] = jnp.zeros(react_in.shape[1:], F32)

    @pl.when(jnp.logical_not(has_high))
    def _():
        for it in range(ITERS):
            halo[it, 1] = jnp.zeros(halo.shape[2:], F32)
        react_in[1] = jnp.zeros(react_in.shape[1:], F32)

    for copy in small:
        copy.wait()
    pl.semaphore_wait(barrier, 3 + rz + (t + n - 1) // n + (2 * n - 2 - t) // n)

    sends = []

    def remote(src, dst, s, q, device):
        return pltpu.make_async_remote_copy(
            src_ref=src, dst_ref=dst, send_sem=s, recv_sem=q,
            device_id=device, device_id_type=pl.DeviceIdType.MESH,
        )

    def launch(*args):
        copy = remote(*args)
        copy.start()
        sends.append(copy)
        return copy

    width = 2 * LANES

    def halo_copies(it, ref):
        down = remote(
            ref.at[:, 0:width], halo.at[it, 1], halo_s.at[it, 0], halo_r.at[it, 1], to(t - 1)
        )
        up = remote(
            ref.at[:, strip - width:strip], halo.at[it, 0],
            halo_s.at[it, 1], halo_r.at[it, 0], to(t + 1),
        )
        return down, up

    def react_copies():
        down = remote(reaction, react_in.at[1], react_s.at[0], react_r.at[1], to(t - 1))
        up = remote(reaction, react_in.at[0], react_s.at[1], react_r.at[0], to(t + 1))
        return down, up

    def start_pair(pair):
        @pl.when(has_low)
        def _():
            pair[0].start()

        @pl.when(has_high)
        def _():
            pair[1].start()

    def arrive_pair(pair):
        @pl.when(has_low)
        def _():
            pair[1].wait_recv()

        @pl.when(has_high)
        def _():
            pair[0].wait_recv()

    def sent_pair(pair):
        @pl.when(has_low)
        def _():
            pair[0].wait_send()

        @pl.when(has_high)
        def _():
            pair[1].wait_send()

    react_pair = react_copies()
    start_pair(react_pair)
    pairs = [halo_copies(0, load), halo_copies(1, field1)]
    start_pair(pairs[0])

    lanes = lane_ids(count)

    def blk(k):
        return slice(k * LANES, (k + 1) * LANES)

    def apply_row(center, above, below, coefficient):
        west = jnp.where(lanes == 0, 0.0, pltpu.roll(center, 1, 1))
        east = jnp.where(lanes == LANES - 1, 0.0, pltpu.roll(center, LANES - 1, 1))
        return (coefficient + 4.0) * center - (above + below + west + east)

    def stencil(it, ref):
        def f(k):
            if k < 0:
                return halo[it, 0][:, blk(k + 2)]
            if k >= rows:
                return halo[it, 1][:, blk(k - rows)]
            return ref[:, blk(k)]

        def coefficient(k):
            if k < 0:
                return react_in[0][rows - 1:rows, :]
            if k >= rows:
                return react_in[1][0:1, :]
            return reaction[k:k + 1, :]

        own = jnp.zeros((count, LANES), F32)
        cross = jnp.zeros((count, LANES), F32)
        for k in range(-1, rows + 1):
            g = apply_row(f(k), f(k - 1), f(k + 1), coefficient(k))
            if k == -1:
                g = jnp.where(has_low, g, 0.0)
            if k == rows:
                g = jnp.where(has_high, g, 0.0)
            efield[it, :, blk(k + 1)] = g
            if 0 <= k < rows:
                own += g * g
                if it:
                    cross += g * efield[0, :, blk(k + 1)]
        for k in range(rows):
            eetwice[it, :, blk(k)] = apply_row(
                efield[it, :, blk(k + 1)], efield[it, :, blk(k)],
                efield[it, :, blk(k + 2)], reaction[k:k + 1, :],
            )
        return jnp.sum(own, axis=1, keepdims=True), jnp.sum(cross, axis=1, keepdims=True)

    def wide_range(c):
        lo = 0 if c == 0 else LANES + starts[c] * rz * LANES
        return lo, LANES + (starts[c] + chunks[c]) * rz * LANES

    def z_range(c):
        lo = 0 if c == 0 else LANES + starts[c] * LANES
        return lo, LANES + (starts[c] + chunks[c]) * LANES

    def out_range(c):
        lo = starts[c] * rz * LANES
        hi = lo + chunks[c] * rz * LANES + (rz * LANES if c == last else 0)
        return lo, hi

    def iteration(it, ref):
        sem = lambda c, k: (sems_s.at[it, c, k], sems_r.at[it, c, k])
        esem = lambda k: (e_s.at[it, k], e_r.at[it, k])
        inflight = {}
        state = {}

        def put_wide(lo, hi, value):
            shaped = value.reshape(4, ROWS16, hi - lo)
            pred32[:, :, lo:hi] = shaped
            return shaped

        def product(c):
            if it == 0:
                loads[c].wait()
            lo = LANES + starts[c] * rz * LANES
            hi = lo + chunks[c] * rz * LANES
            s_lo, s_hi = spans[c]
            mid = lo + s_hi - s_lo
            if mid > lo:
                part = jnp.dot(
                    state["lowered"], sens[:, s_lo:s_hi], preferred_element_type=F32
                )
                send_a[it, :, :, lo:mid] = put_wide(lo, mid, part).astype(BF16)
            if mid < hi:
                rest = put_wide(mid, hi, jnp.zeros((count, hi - mid), F32))
                send_a[it, :, :, mid:hi] = rest.astype(BF16)
            if c == 0:
                whole = ref[...]
                square = jnp.sum(whole * whole, axis=1, keepdims=True)
                send_a[it, :, :, 0:LANES] = encode(put_wide(0, LANES, spread(count, {0: square})))
            lo, hi = wide_range(c)
            for k in range(3):
                inflight["a", c, k] = launch(
                    send_a.at[it, g + steps_xy[k], :, lo:hi], recv_a.at[it, k, :, lo:hi],
                    *sem(c, k), to(xy_peers[k]),
                )

        def sum_xy(c):
            for k in range(3):
                inflight["a", c, k].wait_recv()
            lo = LANES + starts[c] * rz * LANES
            u = chunks[c] * LANES
            hi = lo + rz * u
            value = pred32[g, :, lo:hi]
            for k in (1, 2, 0):
                value += recv_a[it, k, :, lo:hi].astype(F32)
            sum_z[:, lo:hi] = value
            z_lo, z_hi = z_range(c)
            for j in range(rz):
                send_z[it, j, :, z_hi - u:z_hi] = value[:, j * u:(j + 1) * u]
            if c == 0:
                value = pred32[g, :, 0:LANES]
                for k in (1, 2, 0):
                    value += decode(recv_a[it, k, :, 0:LANES])
                sum_z[:, 0:LANES] = value
                for j in range(rz):
                    send_z[it, j, :, 0:LANES] = value
            for k in range(1, rz):
                inflight["z", c, k] = launch(
                    send_z.at[it, (z + k) % rz, :, z_lo:z_hi], recv_z.at[it, k - 1, :, z_lo:z_hi],
                    *sem(c, 2 + k), to(z_peers[k - 1]),
                )

        def smooth_part():
            if it:
                start_pair(pairs[it])

        def smooth_xy():
            arrive_pair(pairs[it])
            if it == 0:
                arrive_pair(react_pair)
            own, cross = stencil(it, ref)
            value = spread(count, {1: own, 3: cross})
            efull[...] = value
            state["e"] = efull[pl.ds(pl.multiple_of(r * half, half), half), :]
            esend_a[it] = encode(state["e"])
            for k in range(3):
                inflight["ea", k] = launch(
                    esend_a.at[it], erecv_a.at[it, k], *esem(k), to(xy_peers[k])
                )

        def smooth_z():
            for k in range(3):
                inflight["ea", k].wait_recv()
            for k in (1, 2, 0):
                state["e"] += decode(erecv_a[it, k])
            esend_z[it] = encode(state["e"])
            for k in range(1, rz):
                inflight["ez", k] = launch(
                    esend_z.at[it], erecv_z.at[it, k - 1], *esem(2 + k), to(z_peers[k - 1])
                )

        def smooth_all():
            for k in range(1, rz):
                inflight["ez", k].wait_recv()
                state["e"] += decode(erecv_z[it, k - 1])

        def weigh(c):
            for k in range(1, rz):
                inflight["z", c, k].wait_recv()
            u = chunks[c] * LANES
            z_hi = z_range(c)[1]
            z_lo = z_hi - u
            column = pl.multiple_of(starts[c] * rz * LANES + z * u, LANES)
            own = sum_z[:, pl.ds(pl.multiple_of(LANES + column, LANES), u)]
            for k in range(1, rz):
                own += recv_z[it, k - 1, :, z_lo:z_hi]
            if c == 0:
                fresh = sum_z[:, 0:LANES]
                for k in range(1, rz):
                    fresh += recv_z[it, k - 1, :, 0:LANES]
                state["fresh"] = fresh[:, 0:1]
                if it:
                    state["beta"] = state["fresh"] / scal[g, :, 0:1]
            if it == 0:
                pred0[:, starts[c] * LANES:starts[c] * LANES + u] = own
            else:
                own += state["beta"] * pred0[:, starts[c] * LANES:starts[c] * LANES + u]
            scaled = prec[:, pl.ds(column, u)] * own
            wb[it, g, :, pl.ds(column, u)] = scaled.astype(BF16)
            ref_own = wb.at[it, g, :, pl.ds(column, u)]
            for k in range(1, rz):
                inflight["gz", c, k] = launch(
                    ref_own, ref_own, *sem(c, rz + 1 + k), to(z_peers[k - 1])
                )
            curved = jnp.sum(scaled * own, axis=1, keepdims=True)
            state["curved"] = curved if c == 0 else state["curved"] + curved
            if c == last:
                place = pl.multiple_of(total + z * LANES, LANES)
                wb[it, g, :, pl.ds(place, LANES)] = encode(spread(
                    ROWS16, {0: state["fresh"] * (1.0 / (2 * rz)), 2: state["curved"]},
                ))
                ref_own = wb.at[it, g, :, pl.ds(place, LANES)]
                for k in range(1, rz):
                    inflight["gs", k] = launch(
                        ref_own, ref_own, *sem(c, 2 * rz + k), to(z_peers[k - 1])
                    )

        def hand_on(c):
            for k in range(1, rz):
                inflight["gz", c, k].wait_recv()
                if c == last:
                    inflight["gs", k].wait_recv()
            lo, hi = out_range(c)
            piece = wb.at[it, g, :, lo:hi]
            for k in range(3):
                inflight["g", c, k] = launch(piece, piece, *sem(c, 3 * rz + k), to(xy_peers[k]))

        def back(c):
            for k in range(3):
                inflight["g", c, k].wait_recv()
            lo, hi = spans[c]
            if hi > lo:
                left = wb[it, :, :, lo:hi].reshape(count, hi - lo)
                part = lax.dot_general(
                    left, sens[:, lo:hi], (((1,), (1,)), ((), ())), preferred_element_type=F32
                )
                if c == 0:
                    core_send[it, :, 0:strip] = part
                else:
                    core_send[it, :, 0:strip] += part

        def meet():
            sums = jnp.zeros((count, LANES), F32)
            for j in range(rz):
                piece = wb[it, :, :, total + j * LANES:total + (j + 1) * LANES]
                sums += decode(piece.reshape(count, LANES))
            core_send[it, :, strip:strip + LANES] = sums
            core_send[it, pl.ds(pl.multiple_of(r * half, half), half), strip:strip + LANES] += state["e"]
            copy = launch(
                core_send.at[it], core_recv.at[it], core_s.at[it], core_r.at[it], (t, 1 - r)
            )
            copy.wait_recv()

        state["lowered"] = ref[...].astype(BF16)
        each = range(len(chunks))
        for c in each:
            product(c)
        smooth_part()
        for c in each:
            sum_xy(c)
        smooth_xy()
        for c in each:
            weigh(c)
        smooth_z()
        for c in each:
            hand_on(c)
        smooth_all()
        for c in each:
            back(c)
        meet()
        sums = core_send[it, :, strip:strip + LANES] + core_recv[it, :, strip:strip + LANES]
        scal[...] = sums.reshape(4, ROWS16, LANES)
        return sums

    def back_of(it, k):
        return core_send[it, :, blk(k)] + core_recv[it, :, blk(k)]

    sums0 = iteration(0, load)
    alpha0 = sums0[:, 0:1] / (sums0[:, 1:2] + sums0[:, 2:3])
    for k in range(rows):
        field1[:, blk(k)] = load[:, blk(k)] - alpha0 * (back_of(0, k) + eetwice[0, :, blk(k)])
    sums1 = iteration(1, field1)
    beta = sums1[:, 0:1] / sums0[:, 0:1]
    smooth = sums1[:, 1:2] + 2.0 * beta * sums1[:, 3:4] + beta * beta * sums0[:, 1:2]
    alpha1 = sums1[:, 0:1] / (smooth + sums1[:, 2:3])
    for k in range(rows):
        first, second = load[:, blk(k)], field1[:, blk(k)]
        image = back_of(1, k) + (eetwice[1, :, blk(k)] + beta * eetwice[0, :, blk(k)])
        sol_out[:, blk(k)] = alpha0 * first + alpha1 * (second + beta * first)
        res_out[:, blk(k)] = second - alpha1 * image
    for copy in sends:
        copy.wait_send()
    for pair in [react_pair] + pairs:
        sent_pair(pair)


def per_device(n, sensitivity, precision, reaction, load):
    count, strip = load.shape
    rows = reaction.shape[0]
    obs = sensitivity.shape[1]
    rz = n // 4
    units = -(-obs // (rz * LANES))
    chunks = SPLIT if sum(SPLIT) == units else (units,)
    total = units * rz * LANES
    padded = jnp.pad(precision, (0, total - obs)).reshape(1, total)
    wide, narrow = total + LANES, (units + 1) * LANES
    slots = 3 * rz + 3
    vm = pltpu.VMEM
    dma = pltpu.SemaphoreType.DMA
    out = jax.ShapeDtypeStruct(load.shape, F32)
    return pl.pallas_call(
        functools.partial(kernel, n, chunks),
        out_shape=(out, out),
        in_specs=[pl.BlockSpec(memory_space=pl.ANY)] * 4,
        out_specs=(pl.BlockSpec(memory_space=vm),) * 2,
        scratch_shapes=[
            vm(sensitivity.shape, BF16),
            vm(padded.shape, F32),
            vm(reaction.shape, F32),
            vm(load.shape, F32),
            vm((2, rows, LANES), F32),
            vm((ITERS, 2, count, 2 * LANES), F32),
            vm((count, strip), F32),
            vm((ITERS, count, strip + 2 * LANES), F32),
            vm((ITERS, count, strip), F32),
            vm((4, ROWS16, wide), F32),
            vm((ITERS, 4, ROWS16, wide), BF16),
            vm((ITERS, 3, ROWS16, wide), BF16),
            vm((ROWS16, wide), F32),
            vm((ITERS, rz, ROWS16, narrow), F32),
            vm((ITERS, rz - 1, ROWS16, narrow), F32),
            vm((ROWS16, units * LANES), F32),
            vm((ITERS, 4, ROWS16, total + rz * LANES), BF16),
            vm((ITERS, count, strip + LANES), F32),
            vm((ITERS, count, strip + LANES), F32),
            vm((4, ROWS16, LANES), F32),
            vm((ITERS, count // 2, LANES), BF16),
            vm((ITERS, 3, count // 2, LANES), BF16),
            vm((ITERS, count // 2, LANES), BF16),
            vm((ITERS, rz - 1, count // 2, LANES), BF16),
            vm((count, LANES), F32),
            dma((len(chunks) + 3,)),
            dma((ITERS, len(chunks), slots)),
            dma((ITERS, len(chunks), slots)),
            dma((ITERS, 2)),
            dma((ITERS, 2)),
            dma((2,)),
            dma((2,)),
            dma((ITERS,)),
            dma((ITERS,)),
            dma((ITERS, 2 + rz)),
            dma((ITERS, 2 + rz)),
        ],
        compiler_params=pltpu.CompilerParams(
            collective_id=0, has_side_effects=True, vmem_limit_bytes=48 * 2**20
        ),
    )(sensitivity, padded, reaction, load)


def solution(mesh):
    placed = (P("tile", "rhs"), P("rhs"), P("tile", None), P(None, "tile"))
    return jax.shard_map(
        functools.partial(per_device, mesh.shape["tile"]),
        mesh=mesh,
        in_specs=placed,
        out_specs=(P(None, "tile"), P(None, "tile")),
        check_vma=False,
    )
```

```python
import functools

import jax
import jax.numpy as jnp
from jax import lax
from jax.experimental import pallas as pl
from jax.experimental.pallas import tpu as pltpu
from jax.sharding import PartitionSpec as P

ITERS = 2
LANES = 128
ROWS16 = 16
SPLIT = (1, 2, 2)
F32, BF16 = jnp.float32, jnp.bfloat16


def lane_ids(rows):
    return lax.broadcasted_iota(jnp.int32, (rows, LANES), 1)


def encode(value):
    high = value.astype(BF16).astype(F32)
    lanes = lax.broadcasted_iota(jnp.int32, value.shape, value.ndim - 1)
    return jnp.where(lanes < LANES // 2, high, value - high).astype(BF16)


def decode(piece):
    wide = piece.astype(F32)
    return wide + pltpu.roll(wide, LANES // 2, wide.ndim - 1)


def spread(rows, columns):
    lanes = lane_ids(rows) % (LANES // 2)
    out = jnp.zeros((rows, LANES), F32)
    for lane, column in columns.items():
        out = jnp.where(lanes == lane, column, out)
    return out


def kernel(
    n, chunks, sens_hbm, prec_hbm, reaction_hbm, load_hbm, sol_out, res_out,
    sens, prec, reaction, load, react_in, halo, field1, efield, eetwice,
    pred32, send_a, recv_a, sum_z, send_z, recv_z, pred0, wb, core_send, core_recv, scal,
    esend_a, erecv_a, esend_z, erecv_z, efull,
    load_sem, sems_s, sems_r, halo_s, halo_r, react_s, react_r, core_s, core_r, e_s, e_r,
):
    t = lax.axis_index("tile")
    r = lax.axis_index("rhs")
    rz = n // 4
    x, y, z, g = t % 2, (t // 2) % 2, t // 4, t % 4
    steps_xy = (3 - 2 * x - 4 * y, 1 - 2 * x, 2 - 4 * y)
    count, strip = load.shape
    half = count // 2
    rows = reaction.shape[0]
    obs = sens.shape[1]
    total = sum(chunks) * rz * LANES
    last = len(chunks) - 1
    has_low, has_high = t > 0, t < n - 1

    def to(tile):
        return (tile, r)

    small = []
    for at, (src, dst) in enumerate(((load_hbm, load), (prec_hbm, prec), (reaction_hbm, reaction))):
        copy = pltpu.make_async_copy(src, dst, load_sem.at[len(chunks) + at])
        copy.start()
        small.append(copy)
    starts = [sum(chunks[:c]) for c in range(len(chunks))]
    spans = []
    loads = []
    for c, u in enumerate(chunks):
        lo = min(starts[c] * rz * LANES, obs)
        hi = min((starts[c] + u) * rz * LANES, obs)
        spans.append((lo, hi))
        copy = pltpu.make_async_copy(
            sens_hbm.at[:, lo:hi], sens.at[:, lo:hi], load_sem.at[c]
        )
        copy.start()
        loads.append(copy)

    barrier = pltpu.get_barrier_semaphore()

    def greet(device):
        pl.semaphore_signal(
            barrier, inc=1, device_id=device, device_id_type=pl.DeviceIdType.MESH
        )

    greet((t, 1 - r))
    xy_peers = [t + step for step in steps_xy]
    z_peers = [((z + k) % rz) * 4 + g for k in range(1, rz)]
    for peer in xy_peers + z_peers:
        greet(to(peer))

    @pl.when(has_low)
    def _():
        greet(to(t - 1))

    @pl.when(has_high)
    def _():
        greet(to(t + 1))

    @pl.when(jnp.logical_not(has_low))
    def _():
        for it in range(ITERS):
            halo[it, 0] = jnp.zeros(halo.shape[2:], F32)
        react_in[0] = jnp.zeros(react_in.shape[1:], F32)

    @pl.when(jnp.logical_not(has_high))
    def _():
        for it in range(ITERS):
            halo[it, 1] = jnp.zeros(halo.shape[2:], F32)
        react_in[1] = jnp.zeros(react_in.shape[1:], F32)

    for copy in small:
        copy.wait()
    pl.semaphore_wait(barrier, 3 + rz + (t + n - 1) // n + (2 * n - 2 - t) // n)

    sends = []

    def remote(src, dst, s, q, device):
        return pltpu.make_async_remote_copy(
            src_ref=src, dst_ref=dst, send_sem=s, recv_sem=q,
            device_id=device, device_id_type=pl.DeviceIdType.MESH,
        )

    def launch(*args):
        copy = remote(*args)
        copy.start()
        sends.append(copy)
        return copy

    width = 2 * LANES

    def halo_copies(it, ref):
        down = remote(
            ref.at[:, 0:width], halo.at[it, 1], halo_s.at[it, 0], halo_r.at[it, 1], to(t - 1)
        )
        up = remote(
            ref.at[:, strip - width:strip], halo.at[it, 0],
            halo_s.at[it, 1], halo_r.at[it, 0], to(t + 1),
        )
        return down, up

    def react_copies():
        down = remote(reaction, react_in.at[1], react_s.at[0], react_r.at[1], to(t - 1))
        up = remote(reaction, react_in.at[0], react_s.at[1], react_r.at[0], to(t + 1))
        return down, up

    def start_pair(pair):
        @pl.when(has_low)
        def _():
            pair[0].start()

        @pl.when(has_high)
        def _():
            pair[1].start()

    def arrive_pair(pair):
        @pl.when(has_low)
        def _():
            pair[1].wait_recv()

        @pl.when(has_high)
        def _():
            pair[0].wait_recv()

    def sent_pair(pair):
        @pl.when(has_low)
        def _():
            pair[0].wait_send()

        @pl.when(has_high)
        def _():
            pair[1].wait_send()

    react_pair = react_copies()
    start_pair(react_pair)
    pairs = [halo_copies(0, load), halo_copies(1, field1)]
    start_pair(pairs[0])

    lanes = lane_ids(count)

    def blk(k):
        return slice(k * LANES, (k + 1) * LANES)

    def apply_row(center, above, below, coefficient):
        west = jnp.where(lanes == 0, 0.0, pltpu.roll(center, 1, 1))
        east = jnp.where(lanes == LANES - 1, 0.0, pltpu.roll(center, LANES - 1, 1))
        return (coefficient + 4.0) * center - (above + below + west + east)

    def stencil(it, ref):
        def f(k):
            if k < 0:
                return halo[it, 0][:, blk(k + 2)]
            if k >= rows:
                return halo[it, 1][:, blk(k - rows)]
            return ref[:, blk(k)]

        def coefficient(k):
            if k < 0:
                return react_in[0][rows - 1:rows, :]
            if k >= rows:
                return react_in[1][0:1, :]
            return reaction[k:k + 1, :]

        own = jnp.zeros((count, LANES), F32)
        cross = jnp.zeros((count, LANES), F32)
        for k in range(-1, rows + 1):
            g = apply_row(f(k), f(k - 1), f(k + 1), coefficient(k))
            if k == -1:
                g = jnp.where(has_low, g, 0.0)
            if k == rows:
                g = jnp.where(has_high, g, 0.0)
            efield[it, :, blk(k + 1)] = g
            if 0 <= k < rows:
                own += g * g
                if it:
                    cross += g * efield[0, :, blk(k + 1)]
        for k in range(rows):
            eetwice[it, :, blk(k)] = apply_row(
                efield[it, :, blk(k + 1)], efield[it, :, blk(k)],
                efield[it, :, blk(k + 2)], reaction[k:k + 1, :],
            )
        return jnp.sum(own, axis=1, keepdims=True), jnp.sum(cross, axis=1, keepdims=True)

    def wide_range(c):
        lo = 0 if c == 0 else LANES + starts[c] * rz * LANES
        return lo, LANES + (starts[c] + chunks[c]) * rz * LANES

    def z_range(c):
        lo = 0 if c == 0 else LANES + starts[c] * LANES
        return lo, LANES + (starts[c] + chunks[c]) * LANES

    def out_range(c):
        lo = starts[c] * rz * LANES
        hi = lo + chunks[c] * rz * LANES + (rz * LANES if c == last else 0)
        return lo, hi

    def iteration(it, ref):
        sem = lambda c, k: (sems_s.at[it, c, k], sems_r.at[it, c, k])
        esem = lambda k: (e_s.at[it, k], e_r.at[it, k])
        inflight = {}
        state = {}

        def put_wide(lo, hi, value):
            shaped = value.reshape(4, ROWS16, hi - lo)
            pred32[:, :, lo:hi] = shaped
            return shaped

        def product(c):
            if it == 0:
                loads[c].wait()
            lo = LANES + starts[c] * rz * LANES
            hi = lo + chunks[c] * rz * LANES
            s_lo, s_hi = spans[c]
            mid = lo + s_hi - s_lo
            if mid > lo:
                part = jnp.dot(
                    state["lowered"], sens[:, s_lo:s_hi], preferred_element_type=F32
                )
                send_a[it, :, :, lo:mid] = put_wide(lo, mid, part).astype(BF16)
            if mid < hi:
                rest = put_wide(mid, hi, jnp.zeros((count, hi - mid), F32))
                send_a[it, :, :, mid:hi] = rest.astype(BF16)
            if c == 0:
                whole = ref[...]
                square = jnp.sum(whole * whole, axis=1, keepdims=True)
                send_a[it, :, :, 0:LANES] = encode(put_wide(0, LANES, spread(count, {0: square})))
            lo, hi = wide_range(c)
            for k in range(3):
                inflight["a", c, k] = launch(
                    send_a.at[it, g + steps_xy[k], :, lo:hi], recv_a.at[it, k, :, lo:hi],
                    *sem(c, k), to(xy_peers[k]),
                )

        def sum_xy(c):
            for k in range(3):
                inflight["a", c, k].wait_recv()
            lo = LANES + starts[c] * rz * LANES
            u = chunks[c] * LANES
            hi = lo + rz * u
            value = pred32[g, :, lo:hi]
            for k in (1, 2, 0):
                value += recv_a[it, k, :, lo:hi].astype(F32)
            sum_z[:, lo:hi] = value
            z_lo, z_hi = z_range(c)
            for j in range(rz):
                send_z[it, j, :, z_hi - u:z_hi] = value[:, j * u:(j + 1) * u]
            if c == 0:
                value = pred32[g, :, 0:LANES]
                for k in (1, 2, 0):
                    value += decode(recv_a[it, k, :, 0:LANES])
                sum_z[:, 0:LANES] = value
                for j in range(rz):
                    send_z[it, j, :, 0:LANES] = value
            for k in range(1, rz):
                inflight["z", c, k] = launch(
                    send_z.at[it, (z + k) % rz, :, z_lo:z_hi], recv_z.at[it, k - 1, :, z_lo:z_hi],
                    *sem(c, 2 + k), to(z_peers[k - 1]),
                )

        def smooth_part():
            if it:
                start_pair(pairs[it])

        def smooth_xy():
            arrive_pair(pairs[it])
            if it == 0:
                arrive_pair(react_pair)
            own, cross = stencil(it, ref)
            value = spread(count, {1: own, 3: cross})
            efull[...] = value
            state["e"] = efull[pl.ds(pl.multiple_of(r * half, half), half), :]
            esend_a[it] = encode(state["e"])
            for k in range(3):
                inflight["ea", k] = launch(
                    esend_a.at[it], erecv_a.at[it, k], *esem(k), to(xy_peers[k])
                )

        def smooth_z():
            for k in range(3):
                inflight["ea", k].wait_recv()
            for k in (1, 2, 0):
                state["e"] += decode(erecv_a[it, k])
            esend_z[it] = encode(state["e"])
            for k in range(1, rz):
                inflight["ez", k] = launch(
                    esend_z.at[it], erecv_z.at[it, k - 1], *esem(2 + k), to(z_peers[k - 1])
                )

        def smooth_all():
            for k in range(1, rz):
                inflight["ez", k].wait_recv()
                state["e"] += decode(erecv_z[it, k - 1])

        def weigh(c):
            for k in range(1, rz):
                inflight["z", c, k].wait_recv()
            u = chunks[c] * LANES
            z_hi = z_range(c)[1]
            z_lo = z_hi - u
            column = pl.multiple_of(starts[c] * rz * LANES + z * u, LANES)
            own = sum_z[:, pl.ds(pl.multiple_of(LANES + column, LANES), u)]
            for k in range(1, rz):
                own += recv_z[it, k - 1, :, z_lo:z_hi]
            if c == 0:
                fresh = sum_z[:, 0:LANES]
                for k in range(1, rz):
                    fresh += recv_z[it, k - 1, :, 0:LANES]
                state["fresh"] = fresh[:, 0:1]
                if it:
                    state["beta"] = state["fresh"] / scal[g, :, 0:1]
            if it == 0:
                pred0[:, starts[c] * LANES:starts[c] * LANES + u] = own
            else:
                own += state["beta"] * pred0[:, starts[c] * LANES:starts[c] * LANES + u]
            scaled = prec[:, pl.ds(column, u)] * own
            wb[it, g, :, pl.ds(column, u)] = scaled.astype(BF16)
            ref_own = wb.at[it, g, :, pl.ds(column, u)]
            for k in range(1, rz):
                inflight["gz", c, k] = launch(
                    ref_own, ref_own, *sem(c, rz + 1 + k), to(z_peers[k - 1])
                )
            curved = jnp.sum(scaled * own, axis=1, keepdims=True)
            state["curved"] = curved if c == 0 else state["curved"] + curved
            if c == last:
                place = pl.multiple_of(total + z * LANES, LANES)
                wb[it, g, :, pl.ds(place, LANES)] = encode(spread(
                    ROWS16, {0: state["fresh"] * (1.0 / (2 * rz)), 2: state["curved"]},
                ))
                ref_own = wb.at[it, g, :, pl.ds(place, LANES)]
                for k in range(1, rz):
                    inflight["gs", k] = launch(
                        ref_own, ref_own, *sem(c, 2 * rz + k), to(z_peers[k - 1])
                    )

        def hand_on(c):
            for k in range(1, rz):
                inflight["gz", c, k].wait_recv()
                if c == last:
                    inflight["gs", k].wait_recv()
            lo, hi = out_range(c)
            piece = wb.at[it, g, :, lo:hi]
            for k in range(3):
                inflight["g", c, k] = launch(piece, piece, *sem(c, 3 * rz + k), to(xy_peers[k]))

        def back(c):
            for k in range(3):
                inflight["g", c, k].wait_recv()
            lo, hi = spans[c]
            if hi > lo:
                left = wb[it, :, :, lo:hi].reshape(count, hi - lo)
                part = lax.dot_general(
                    left, sens[:, lo:hi], (((1,), (1,)), ((), ())), preferred_element_type=F32
                )
                if c == 0:
                    core_send[it, :, 0:strip] = part
                else:
                    core_send[it, :, 0:strip] += part

        def meet():
            sums = jnp.zeros((count, LANES), F32)
            for j in range(rz):
                piece = wb[it, :, :, total + j * LANES:total + (j + 1) * LANES]
                sums += decode(piece.reshape(count, LANES))
            core_send[it, :, strip:strip + LANES] = sums
            core_send[it, pl.ds(pl.multiple_of(r * half, half), half), strip:strip + LANES] += state["e"]
            copy = launch(
                core_send.at[it], core_recv.at[it], core_s.at[it], core_r.at[it], (t, 1 - r)
            )
            copy.wait_recv()

        state["lowered"] = ref[...].astype(BF16)
        each = range(len(chunks))
        for c in each:
            product(c)
        smooth_part()
        for c in each:
            sum_xy(c)
        smooth_xy()
        for c in each:
            weigh(c)
        smooth_z()
        for c in each:
            hand_on(c)
        smooth_all()
        for c in each:
            back(c)
        meet()
        sums = core_send[it, :, strip:strip + LANES] + core_recv[it, :, strip:strip + LANES]
        scal[...] = sums.reshape(4, ROWS16, LANES)
        return sums

    def back_of(it, k):
        return core_send[it, :, blk(k)] + core_recv[it, :, blk(k)]

    sums0 = iteration(0, load)
    alpha0 = sums0[:, 0:1] / (sums0[:, 1:2] + sums0[:, 2:3])
    for k in range(rows):
        field1[:, blk(k)] = load[:, blk(k)] - alpha0 * (back_of(0, k) + eetwice[0, :, blk(k)])
    sums1 = iteration(1, field1)
    beta = sums1[:, 0:1] / sums0[:, 0:1]
    smooth = sums1[:, 1:2] + 2.0 * beta * sums1[:, 3:4] + beta * beta * sums0[:, 1:2]
    alpha1 = sums1[:, 0:1] / (smooth + sums1[:, 2:3])
    for k in range(rows):
        first, second = load[:, blk(k)], field1[:, blk(k)]
        image = back_of(1, k) + (eetwice[1, :, blk(k)] + beta * eetwice[0, :, blk(k)])
        sol_out[:, blk(k)] = alpha0 * first + alpha1 * (second + beta * first)
        res_out[:, blk(k)] = second - alpha1 * image
    for copy in sends:
        copy.wait_send()
    for pair in [react_pair] + pairs:
        sent_pair(pair)


def per_device(n, sensitivity, precision, reaction, load):
    count, strip = load.shape
    rows = reaction.shape[0]
    obs = sensitivity.shape[1]
    rz = n // 4
    units = -(-obs // (rz * LANES))
    chunks = SPLIT if sum(SPLIT) == units else (units,)
    total = units * rz * LANES
    padded = jnp.pad(precision, (0, total - obs)).reshape(1, total)
    wide, narrow = total + LANES, (units + 1) * LANES
    slots = 3 * rz + 3
    vm = pltpu.VMEM
    dma = pltpu.SemaphoreType.DMA
    out = jax.ShapeDtypeStruct(load.shape, F32)
    return pl.pallas_call(
        functools.partial(kernel, n, chunks),
        out_shape=(out, out),
        in_specs=[pl.BlockSpec(memory_space=pl.ANY)] * 4,
        out_specs=(pl.BlockSpec(memory_space=vm),) * 2,
        scratch_shapes=[
            vm(sensitivity.shape, BF16),
            vm(padded.shape, F32),
            vm(reaction.shape, F32),
            vm(load.shape, F32),
            vm((2, rows, LANES), F32),
            vm((ITERS, 2, count, 2 * LANES), F32),
            vm((count, strip), F32),
            vm((ITERS, count, strip + 2 * LANES), F32),
            vm((ITERS, count, strip), F32),
            vm((4, ROWS16, wide), F32),
            vm((ITERS, 4, ROWS16, wide), BF16),
            vm((ITERS, 3, ROWS16, wide), BF16),
            vm((ROWS16, wide), F32),
            vm((ITERS, rz, ROWS16, narrow), F32),
            vm((ITERS, rz - 1, ROWS16, narrow), F32),
            vm((ROWS16, units * LANES), F32),
            vm((ITERS, 4, ROWS16, total + rz * LANES), BF16),
            vm((ITERS, count, strip + LANES), F32),
            vm((ITERS, count, strip + LANES), F32),
            vm((4, ROWS16, LANES), F32),
            vm((ITERS, count // 2, LANES), BF16),
            vm((ITERS, 3, count // 2, LANES), BF16),
            vm((ITERS, count // 2, LANES), BF16),
            vm((ITERS, rz - 1, count // 2, LANES), BF16),
            vm((count, LANES), F32),
            dma((len(chunks) + 3,)),
            dma((ITERS, len(chunks), slots)),
            dma((ITERS, len(chunks), slots)),
            dma((ITERS, 2)),
            dma((ITERS, 2)),
            dma((2,)),
            dma((2,)),
            dma((ITERS,)),
            dma((ITERS,)),
            dma((ITERS, 2 + rz)),
            dma((ITERS, 2 + rz)),
        ],
        compiler_params=pltpu.CompilerParams(
            collective_id=0, has_side_effects=True, vmem_limit_bytes=48 * 2**20
        ),
    )(sensitivity, padded, reaction, load)


def solution(mesh):
    placed = (P("tile", "rhs"), P("rhs"), P("tile", None), P(None, "tile"))
    return jax.shard_map(
        functools.partial(per_device, mesh.shape["tile"]),
        mesh=mesh,
        in_specs=placed,
        out_specs=(P(None, "tile"), P(None, "tile")),
        check_vma=False,
    )
```
